32 devices in a mesh: brick: 16 (over z, x, core), vec: 2 (over y).
Axes of the slice: x: 2, y: 2, z: 4, core: 2. Of those that a mesh axis runs over, the one named last changes fastest.
Arguments:
- levels: int32 [12, 512, 16, 128], P(None, 'brick'), may hold values from 0 to 255
- start_block: int32 [16, 512, 16, 128], P('vec', 'brick'), may hold values from -8 to 8
Outputs:
- alpha_blocks: float32 [1, 16, 16], replicated
- beta_blocks: float32 [1, 16, 16], replicated
- basis: float32 [16, 512, 16, 128], P('vec', 'brick')
The draws below stay inside these ranges and needn't reach their ends.
All inputs are finite; a program needn't handle non-finite values.
Results may differ from the reference program's by a relative error of at most 0.00026.
Values sent between devices are 32-bit elements; how exact they have to be, the bound alone decides.
A program may use at most 128 MiB of HBM per device.

```python
import math
import jax
import jax.numpy as jnp
from jax import lax

BLOCK = 16
CHANNELS = 12
STEPS = 1
NY = 16
NZ = 128
NX = 512
VOXELS = 1048576


def plant(values, key, smallest, high):
    shape = values.shape
    place = [jax.random.randint(jax.random.fold_in(key, axis), (), 0, shape[axis]) for axis in range(len(shape))]
    values = values.at[tuple(place)].set(smallest)
    longest = shape.index(max(shape))
    place[longest] = (place[longest] + 1) % shape[longest]
    return values.at[tuple(place)].set(high)


def setup_inputs(seed: int = 0) -> dict:
    keys = jax.random.split(jax.random.key(seed), 3)
    levels = plant(jax.random.randint(keys[0], (CHANNELS, NX, NY, NZ), 0, 256), jax.random.fold_in(keys[0], 1), 0, 255).astype(jnp.int32)
    start_block = plant(jax.random.randint(keys[1], (BLOCK, NX, NY, NZ), -8, 9), jax.random.fold_in(keys[1], 1), -8, 8).astype(jnp.int32)
    return dict(levels=levels, start_block=start_block)


offsets_cube = (1, 3, 9, 27)
highest = lax.Precision.HIGHEST

def forward_take(field_in, offset, axis_dim):
    length_dim = field_in.shape[axis_dim]
    widths = [(0, 0)] * field_in.ndim
    widths[axis_dim] = (0, offset)
    return lax.slice_in_dim(jnp.pad(field_in, widths), offset, offset + length_dim, axis=axis_dim)

def backward_put(field_in, offset, axis_dim):
    length_dim = field_in.shape[axis_dim]
    widths = [(0, 0)] * field_in.ndim
    widths[axis_dim] = (offset, 0)
    return lax.slice_in_dim(jnp.pad(field_in, widths), 0, length_dim, axis=axis_dim)

def affinity_apply(field_in, weights):
    result = jnp.zeros_like(field_in)
    for axis_dim in range(3):
        for position, offset in enumerate(offsets_cube):
            channel = weights[4 * axis_dim + position]
            result = result + channel * forward_take(field_in, offset, axis_dim) + backward_put(channel * field_in, offset, axis_dim)
    return result

def inner_of(left_rows, right_rows):
    return jnp.einsum('in,jn->ij', left_rows, right_rows, precision=highest)

def reference(levels, start_block):
    weights = (levels.astype(jnp.float32) + 0.5) / 256.0
    degree = affinity_apply(jnp.ones(levels.shape[1:], jnp.float32), weights) + 1.0
    inv_root = lax.rsqrt(degree)

    def half_step(column):
        return 0.5 * (column + inv_root * affinity_apply(inv_root * column, weights))

    def filtered(column):
        return half_step(half_step(column))
    shape_grid = start_block.shape
    start_work = start_block.astype(jnp.float32).reshape(BLOCK, -1)
    lower_factor = jnp.linalg.cholesky(inner_of(start_work, start_work))
    current = lax.linalg.triangular_solve(lower_factor, start_work, left_side=True, lower=True)
    known_rows = current
    alpha_list = []
    beta_list = []
    for sweep_index in range(STEPS):
        image_block = lax.map(filtered, current.reshape(shape_grid)).reshape(BLOCK, -1)
        coeffs = inner_of(image_block, known_rows)
        residual = image_block - jnp.einsum('ij,jn->in', coeffs, known_rows, precision=highest)
        gram_matrix = inner_of(residual, residual)
        lower_factor = jnp.linalg.cholesky(gram_matrix)
        following = lax.linalg.triangular_solve(lower_factor, residual, left_side=True, lower=True)
        alpha_list.append(coeffs[:, :BLOCK])
        beta_list.append(lower_factor)
        known_rows = jnp.concatenate([following, current], axis=0)
        current = following
    basis = current.reshape(shape_grid) * math.sqrt(VOXELS)
    return (jnp.stack(alpha_list), jnp.stack(beta_list), basis)
```

```python
import functools
import math

import jax
import jax.numpy as jnp
from jax import lax
from jax.experimental import pallas as pl
from jax.experimental.pallas import tpu as pltpu
from jax.sharding import PartitionSpec as P

offsets_cube = (1, 3, 9, 27)
deepest = 27
highest = lax.Precision.HIGHEST
GROUPS = 2
MESH = pl.DeviceIdType.MESH


def shift_up(value, axis):
    size = lax.axis_size(axis)
    return lax.ppermute(value, axis, [(i, i + 1) for i in range(size - 1)])


def shift_down(value, axis):
    size = lax.axis_size(axis)
    return lax.ppermute(value, axis, [(i + 1, i) for i in range(size - 1)])


def forward_take(field_in, offset, axis_dim):
    length_dim = field_in.shape[axis_dim]
    widths = [(0, 0)] * field_in.ndim
    widths[axis_dim] = (0, offset)
    return lax.slice_in_dim(jnp.pad(field_in, widths), offset, offset + length_dim, axis=axis_dim)


def backward_put(field_in, offset, axis_dim):
    length_dim = field_in.shape[axis_dim]
    widths = [(0, 0)] * field_in.ndim
    widths[axis_dim] = (offset, 0)
    return lax.slice_in_dim(jnp.pad(field_in, widths), 0, length_dim, axis=axis_dim)


def local_planes(field_in, weights, result):
    for axis_dim in (2, 3):
        for position, offset in enumerate(offsets_cube):
            channel = weights[4 * (axis_dim - 1) + position]
            result = (
                result
                + channel * forward_take(field_in, offset, axis_dim)
                + backward_put(channel * field_in, offset, axis_dim)
            )
    return result


def apply_padded(field_in, before, after, weights, lower_ext):
    row_count = field_in.shape[1]
    padded = jnp.concatenate([before, field_in, after], axis=1)
    result = jnp.zeros_like(field_in)
    for position, offset in enumerate(offsets_cube):
        result = (
            result + weights[position] * padded[:, deepest + offset : deepest + offset + row_count]
        )
        result = (
            result
            + lower_ext[position][:row_count]
            * padded[:, deepest - offset : deepest - offset + row_count]
        )
    return local_planes(field_in, weights, result)


def sum_kernel(bricks, vecs, own_ref, out_ref, slots, send_sem, recv_sem):
    brick = lax.axis_index("brick")
    vec = lax.axis_index("vec")
    total = bricks * vecs
    me = brick * vecs + vec

    def peer(step):
        other = lax.rem(me + step, total)
        return (other // vecs, lax.rem(other, vecs))

    barrier = pltpu.get_barrier_semaphore()

    def greet(step, carry):
        pl.semaphore_signal(barrier, inc=1, device_id=peer(step), device_id_type=MESH)
        return carry

    lax.fori_loop(1, total, greet, 0)
    pl.semaphore_wait(barrier, total - 1)

    def copy_of(step):
        return pltpu.make_async_remote_copy(
            src_ref=own_ref,
            dst_ref=slots.at[me],
            send_sem=send_sem.at[step],
            recv_sem=recv_sem.at[step],
            device_id=peer(step),
            device_id_type=MESH,
        )

    def push(step, carry):
        copy_of(step).start()
        return carry

    lax.fori_loop(1, total, push, 0)
    slots[pl.ds(me, 1)] = own_ref[...][None]

    def settle(step, carry):
        copy_of(step).wait()
        return carry

    lax.fori_loop(1, total, settle, 0)
    for half in range(vecs):
        value = slots[half]
        for other in range(1, bricks):
            value = value + slots[other * vecs + half]
        out_ref[half] = value


def all_sum(tile):
    bricks, vecs = lax.axis_size("brick"), lax.axis_size("vec")
    total = bricks * vecs
    return pl.pallas_call(
        functools.partial(sum_kernel, bricks, vecs),
        out_shape=jax.ShapeDtypeStruct((vecs,) + tile.shape, jnp.float32),
        in_specs=[pl.BlockSpec(memory_space=pltpu.VMEM)],
        out_specs=pl.BlockSpec(memory_space=pltpu.VMEM),
        scratch_shapes=[
            pltpu.VMEM((total,) + tile.shape, jnp.float32),
            pltpu.SemaphoreType.DMA((total,)),
            pltpu.SemaphoreType.DMA((total,)),
        ],
        compiler_params=pltpu.CompilerParams(collective_id=0, has_side_effects=True),
        name="sum_blocks",
    )(tile)


def body(levels, start_block):
    own_cols, rows = start_block.shape[:2]
    grid_shape = start_block.shape
    vecs = lax.axis_size("vec")
    vec = lax.axis_index("vec")
    voxel_total = lax.axis_size("brick") * rows * grid_shape[2] * grid_shape[3]
    block = own_cols * vecs

    x = start_block.astype(jnp.float32)
    flat_x = x.reshape(own_cols, -1)
    swap = [(0, 1), (1, 0)]
    weights = (levels.astype(jnp.float32) + 0.5) / 256.0
    tails = jnp.concatenate(
        [weights[k, rows - o :] for k, o in enumerate(offsets_cube)], axis=0
    )
    tails = shift_up(tails, "brick")
    x_before = shift_up(x[:, rows - deepest :], "brick")
    x_after = shift_down(x[:, :deepest], "brick")
    x_other = lax.ppermute(flat_x, "vec", swap)
    lower_ext = []
    start = 0
    for k, o in enumerate(offsets_cube):
        lower_ext.append(jnp.concatenate([tails[start : start + o], weights[k]], axis=0))
        start += o

    def is_edge(value, side):
        keep = lax.axis_index("brick") != side
        return jnp.where(keep, value, 0.0)

    ones_halo = jnp.ones((1, deepest) + grid_shape[2:], jnp.float32)
    unit_field = jnp.ones((1,) + grid_shape[1:], jnp.float32)
    degree = apply_padded(
        unit_field,
        is_edge(ones_halo, 0),
        is_edge(ones_halo, lax.axis_size("brick") - 1),
        weights,
        lower_ext,
    )
    inv_root = lax.rsqrt(degree[0] + 1.0)
    root_before = shift_up(inv_root[rows - deepest :], "brick")
    root_after = shift_down(inv_root[:deepest], "brick")

    size = own_cols // GROUPS
    y_parts, y_sent = [], []
    t_parts = []
    for g in range(GROUPS):
        cols = slice(g * size, (g + 1) * size)
        applied = apply_padded(
            inv_root * x[cols],
            root_before * x_before[cols],
            root_after * x_after[cols],
            weights,
            lower_ext,
        )
        t = 0.5 * (x[cols] + inv_root * applied)
        u = inv_root * t
        t_parts.append(
            (t, u, shift_up(u[:, rows - deepest :], "brick"), shift_down(u[:, :deepest], "brick"))
        )
    for g in range(GROUPS):
        t, u, before, after = t_parts[g]
        y = 0.5 * (t + inv_root * apply_padded(u, before, after, weights, lower_ext))
        y = y.reshape(size, -1)
        y_parts.append(y)
        y_sent.append(lax.ppermute(y, "vec", [(0, 1)]))
    y = jnp.concatenate(y_parts, axis=0)
    y_other = jnp.concatenate(y_sent, axis=0)
    first = vec == 0
    x_low = jnp.where(first, flat_x, x_other)
    x_high = jnp.where(first, x_other, flat_x)
    y_low = jnp.where(first, y, y_other)
    y_high = jnp.where(first, 0.0, y)
    x_all = jnp.concatenate([x_low, x_high], axis=0)
    y_all = jnp.concatenate([y_low, y_high], axis=0)

    def inner(left, right):
        return jnp.einsum("in,jn->ij", left, right, precision=highest)

    tile = jnp.concatenate(
        [inner(flat_x, x_all), inner(y, x_all), inner(y, y_all)], axis=1
    )
    tile = jnp.pad(tile, ((0, 0), (0, (-tile.shape[1]) % 128)))
    sums = all_sum(tile).reshape(block, -1)
    g00 = sums[:, :block]
    g10 = sums[:, block : 2 * block]
    g11 = jnp.tril(sums[:, 2 * block : 3 * block])
    g11 = g11 + jnp.tril(g11, -1).T
    gram = jnp.concatenate(
        [jnp.concatenate([g00, g10.T], axis=1), jnp.concatenate([g10, g11], axis=1)], axis=0
    )
    factor = jnp.linalg.cholesky(gram)
    inverse = lax.linalg.triangular_solve(
        factor, jnp.eye(2 * block, dtype=jnp.float32), left_side=True, lower=True
    )
    mixed = jnp.dot(inverse[:block, :block], factor[block:], precision=highest)
    alpha, beta = mixed[:, :block], mixed[:, block:]
    coeffs = lax.dynamic_slice_in_dim(inverse, block + vec * own_cols, own_cols, 0)
    coeffs = coeffs * math.sqrt(voxel_total)
    stacked = jnp.concatenate([x_all, y_all], axis=0)
    basis = jnp.dot(coeffs, stacked, precision=highest).reshape(grid_shape)
    return alpha[None], beta[None], basis


def solution(mesh):
    return jax.shard_map(
        body,
        mesh=mesh,
        in_specs=(P(None, "brick", None, None), P("vec", "brick", None, None)),
        out_specs=(P(), P(), P("vec", "brick", None, None)),
        check_vma=False,
    )
```

```python
import functools
import math

import jax
import jax.numpy as jnp
from jax import lax
from jax.experimental import pallas as pl
from jax.experimental.pallas import tpu as pltpu
from jax.sharding import PartitionSpec as P

offsets_cube = (1, 3, 9, 27)
deepest = 27
highest = lax.Precision.HIGHEST
MESH = pl.DeviceIdType.MESH


def sum_kernel(bricks, vecs, own_ref, out_ref, slots, send_sem, recv_sem):
    brick = lax.axis_index("brick")
    vec = lax.axis_index("vec")
    total = bricks * vecs
    me = brick * vecs + vec

    def peer(step):
        other = lax.rem(me + step, total)
        return (other // vecs, lax.rem(other, vecs))

    barrier = pltpu.get_barrier_semaphore()

    def greet(step, carry):
        pl.semaphore_signal(barrier, inc=1, device_id=peer(step), device_id_type=MESH)
        return carry

    lax.fori_loop(1, total, greet, 0)
    pl.semaphore_wait(barrier, total - 1)

    def copy_of(step):
        return pltpu.make_async_remote_copy(
            src_ref=own_ref,
            dst_ref=slots.at[me],
            send_sem=send_sem.at[step],
            recv_sem=recv_sem.at[step],
            device_id=peer(step),
            device_id_type=MESH,
        )

    def push(step, carry):
        copy_of(step).start()
        return carry

    lax.fori_loop(1, total, push, 0)
    slots[pl.ds(me, 1)] = own_ref[...][None]

    def settle(step, carry):
        copy_of(step).wait()
        return carry

    lax.fori_loop(1, total, settle, 0)
    for half in range(vecs):
        value = slots[half]
        for other in range(1, bricks):
            value = value + slots[other * vecs + half]
        out_ref[half] = value


def all_sum(tile):
    bricks, vecs = lax.axis_size("brick"), lax.axis_size("vec")
    total = bricks * vecs
    return pl.pallas_call(
        functools.partial(sum_kernel, bricks, vecs),
        out_shape=jax.ShapeDtypeStruct((vecs,) + tile.shape, jnp.float32),
        in_specs=[pl.BlockSpec(memory_space=pltpu.VMEM)],
        out_specs=pl.BlockSpec(memory_space=pltpu.VMEM),
        scratch_shapes=[
            pltpu.VMEM((total,) + tile.shape, jnp.float32),
            pltpu.SemaphoreType.DMA((total,)),
            pltpu.SemaphoreType.DMA((total,)),
        ],
        compiler_params=pltpu.CompilerParams(collective_id=0, has_side_effects=True),
        name="sum_blocks",
    )(tile)


ROW_STEP = 4


def fused_kernel(
    bricks, lev_ref, start_ref, x_ref, xo_ref, y_ref, yo_ref, tile_ref,
    x_low, x_high, u_one, u_two, x_weights, fore, back, root, send_sem, recv_sem,
):
    cols, rows, ny, nz = start_ref.shape
    far = deepest
    step = ROW_STEP
    brick = lax.axis_index("brick")
    vec = lax.axis_index("vec")
    has_low = brick > 0
    has_high = brick < bricks - 1
    low, high = {"brick": brick - 1}, {"brick": brick + 1}
    partner = {"vec": 1 - vec}

    def remote(src, dst, kind, slot, device):
        return pltpu.make_async_remote_copy(
            src_ref=src,
            dst_ref=dst,
            send_sem=send_sem.at[kind, slot],
            recv_sem=recv_sem.at[kind, slot],
            device_id=device,
            device_id_type=MESH,
        )

    def x_up(c):
        return remote(x_ref.at[c, pl.ds(rows - far, far)], x_low.at[c], 0, c, high)

    def x_down(c):
        return remote(x_ref.at[c, pl.ds(0, far)], x_high.at[c], 1, c, low)

    def x_over(c):
        return remote(x_ref.at[c], xo_ref.at[c], 2, c, partner)

    def u_up(c):
        return remote(u_two.at[c, pl.ds(rows, far)], u_two.at[c, pl.ds(0, far)], 3, c, high)

    def u_down(c):
        return remote(
            u_two.at[c, pl.ds(far, far)], u_two.at[c, pl.ds(far + rows, far)], 4, c, low
        )

    def y_over(c):
        return remote(y_ref.at[c], yo_ref.at[c], 5, c, partner)

    def tail_up(k):
        o = offsets_cube[k]
        return remote(
            x_weights.at[k, pl.ds(far + rows - o, o)],
            x_weights.at[k, pl.ds(far - o, o)],
            6,
            k,
            high,
        )

    def root_up():
        return remote(root.at[pl.ds(rows, far)], root.at[pl.ds(0, far)], 6, 4, high)

    def root_down():
        return remote(root.at[pl.ds(far, far)], root.at[pl.ds(far + rows, far)], 6, 5, low)

    barrier = pltpu.get_barrier_semaphore()

    def greet(device):
        pl.semaphore_signal(barrier, inc=1, device_id=device, device_id_type=MESH)

    greet(partner)
    pl.when(has_low)(lambda: greet(low))
    pl.when(has_high)(lambda: greet(high))

    def weights_of(channel, place):
        return (lev_ref[channel, place].astype(jnp.float32) + 0.5) * (1.0 / 256.0)

    def prepare_x(r, carry):
        place = pl.ds(r * step, step)
        for k in range(4):
            x_weights[k, pl.ds(far + r * step, step)] = weights_of(k, place)
        return carry

    lax.fori_loop(0, rows // step, prepare_x, 0)

    def cast(c, carry):
        x_ref[c] = start_ref[c].astype(jnp.float32)
        return carry

    lax.fori_loop(0, cols, cast, 0)
    pl.semaphore_wait(
        barrier, 1 + jnp.where(has_low, 1, 0) + jnp.where(has_high, 1, 0)
    )

    @pl.when(has_high)
    def _():
        for k in range(4):
            tail_up(k).start()

    def push_x(c, carry):
        pl.when(has_high)(lambda: x_up(c).start())
        pl.when(has_low)(lambda: x_down(c).start())
        x_over(c).start()
        return carry

    lax.fori_loop(0, cols, push_x, 0)

    edge = jnp.zeros((far, ny, nz), jnp.float32)

    @pl.when(jnp.logical_not(has_low))
    def _():
        root[pl.ds(0, far)] = edge
        for k in range(4):
            x_weights[k, pl.ds(0, far)] = edge
        for c in range(cols):
            x_low[c] = edge
            u_two[c, pl.ds(0, far)] = edge

    @pl.when(jnp.logical_not(has_high))
    def _():
        root[pl.ds(far + rows, far)] = edge
        for c in range(cols):
            x_high[c] = edge
            u_two[c, pl.ds(far + rows, far)] = edge

    lane = (step, ny, nz)
    along = [lax.broadcasted_iota(jnp.int32, lane, axis) for axis in range(3)]

    def prepare_rest(r, carry):
        place = pl.ds(r * step, step)
        degree = jnp.ones(lane, jnp.float32)
        for axis, length in ((1, ny), (2, nz)):
            for k, o in enumerate(offsets_cube):
                if o >= length:
                    continue
                channel = 4 * (axis - 1) + k
                weight = weights_of(channel + 4, place)
                forward = jnp.where(along[axis] < length - o, weight, 0.0)
                backward = pltpu.roll(forward, o, axis)
                fore[channel, place] = forward
                back[channel, place] = backward
                degree = degree + forward + backward
        root[pl.ds(far + r * step, step)] = degree
        return carry

    lax.fori_loop(0, rows // step, prepare_rest, 0)

    @pl.when(has_low)
    def _():
        for k in range(4):
            tail_up(k).wait_recv()

    limit = jnp.where(has_high, rows + far + 1, rows)

    def prepare_root(r, carry):
        place = pl.ds(far + r * step, step)
        degree = root[place]
        for k, o in enumerate(offsets_cube):
            inside = along[0] + (r * step + o) < limit
            degree = degree + jnp.where(inside, x_weights[k, place], 0.0)
            degree = degree + x_weights[k, pl.ds(far + r * step - o, step)]
        root[place] = lax.rsqrt(degree)
        return carry

    lax.fori_loop(0, rows // step, prepare_root, 0)
    pl.when(has_high)(lambda: root_up().start())
    pl.when(has_low)(lambda: root_down().start())

    def stencil(u_ref, r):
        at = far + r * step
        center = u_ref[pl.ds(at, step)]
        total = jnp.zeros(lane, jnp.float32)
        for k, o in enumerate(offsets_cube):
            total = total + x_weights[k, pl.ds(at, step)] * u_ref[pl.ds(at + o, step)]
            total = total + x_weights[k, pl.ds(at - o, step)] * u_ref[pl.ds(at - o, step)]
        place = pl.ds(r * step, step)
        for axis, length in ((1, ny), (2, nz)):
            for k, o in enumerate(offsets_cube):
                if o >= length:
                    continue
                channel = 4 * (axis - 1) + k
                total = total + fore[channel, place] * pltpu.roll(center, length - o, axis)
                total = total + back[channel, place] * pltpu.roll(center, o, axis)
        return root[pl.ds(at, step)] * total

    pl.when(has_low)(lambda: root_up().wait_recv())
    pl.when(has_high)(lambda: root_down().wait_recv())

    def first_half(c, carry):
        u_one[pl.ds(far, rows)] = root[pl.ds(far, rows)] * x_ref[c]
        pl.when(has_low)(lambda: x_up(c).wait_recv())
        u_one[pl.ds(0, far)] = root[pl.ds(0, far)] * x_low[c]
        pl.when(has_high)(lambda: x_down(c).wait_recv())
        u_one[pl.ds(far + rows, far)] = root[pl.ds(far + rows, far)] * x_high[c]

        def one(r, inner):
            place = pl.ds(r * step, step)
            image = 0.5 * (x_ref[c, place] + stencil(u_one, r))
            y_ref[c, place] = image
            at = pl.ds(far + r * step, step)
            u_two[c, at] = root[at] * image
            return inner

        lax.fori_loop(0, rows // step, one, 0)
        pl.when(has_high)(lambda: u_up(c).start())
        pl.when(has_low)(lambda: u_down(c).start())
        return carry

    lax.fori_loop(0, cols, first_half, 0)

    column = lax.broadcasted_iota(jnp.int32, tile_ref.shape, 1)

    def products(left_ref, right_ref, base, tile, ready=None):
        def one(j, tile):
            if ready is not None:
                ready(j)

            def add(r, total):
                return total + left_ref[:, r] * right_ref[j, r][None]

            total = lax.fori_loop(
                0, rows, add, jnp.zeros((cols, ny, nz), jnp.float32), unroll=2
            )
            value = jnp.sum(jnp.sum(total, axis=1), axis=1, keepdims=True)
            return jnp.where(column == base + j, value, tile)

        return lax.fori_loop(0, cols, one, tile)

    tile = products(x_ref, x_ref, 0, jnp.zeros(tile_ref.shape, jnp.float32))

    def second_half(c, carry):
        pl.when(has_low)(lambda: u_up(c).wait_recv())
        pl.when(has_high)(lambda: u_down(c).wait_recv())

        def one(r, inner):
            place = pl.ds(r * step, step)
            y_ref[c, place] = 0.5 * (y_ref[c, place] + stencil(u_two.at[c], r))
            return inner

        lax.fori_loop(0, rows // step, one, 0)
        pl.when(vec == 0)(lambda: y_over(c).start())
        return carry

    lax.fori_loop(0, cols, second_half, 0)
    tile = products(x_ref, xo_ref, cols, tile, lambda j: x_over(j).wait_recv())
    tile = products(y_ref, x_ref, 2 * cols, tile)
    tile = products(y_ref, xo_ref, 3 * cols, tile)
    tile = products(y_ref, y_ref, 4 * cols, tile)
    tile_ref[...] = tile

    @pl.when(vec == 1)
    def _():
        tile_ref[...] = products(
            y_ref, yo_ref, 5 * cols, tile_ref[...], lambda j: y_over(j).wait_recv()
        )

    @pl.when(vec == 0)
    def _():
        for c in range(cols):
            yo_ref[c] = jnp.zeros((rows, ny, nz), jnp.float32)

    def finish(c, carry):
        x_over(c).wait_send()

        @pl.when(has_high)
        def _():
            x_up(c).wait_send()
            u_up(c).wait_send()

        @pl.when(has_low)
        def _():
            x_down(c).wait_send()
            u_down(c).wait_send()

        pl.when(vec == 0)(lambda: y_over(c).wait_send())
        return carry

    lax.fori_loop(0, cols, finish, 0)

    @pl.when(has_high)
    def _():
        for k in range(4):
            tail_up(k).wait_send()
        root_up().wait_send()

    pl.when(has_low)(lambda: root_down().wait_send())


def fused(levels, start_block):
    cols, rows, ny, nz = start_block.shape
    far = deepest
    field = jax.ShapeDtypeStruct(start_block.shape, jnp.float32)
    in_vmem = pl.BlockSpec(memory_space=pltpu.VMEM)
    plane = (ny, nz)

    def room(*lead):
        return pltpu.VMEM(lead + plane, jnp.float32)

    return pl.pallas_call(
        functools.partial(fused_kernel, lax.axis_size("brick")),
        out_shape=(field,) * 4 + (jax.ShapeDtypeStruct((cols, 128), jnp.float32),),
        in_specs=[in_vmem] * 2,
        out_specs=(in_vmem,) * 5,
        scratch_shapes=[
            room(cols, far),
            room(cols, far),
            room(rows + 2 * far),
            room(cols, rows + 2 * far),
            room(4, rows + far),
            room(8, rows),
            room(8, rows),
            room(rows + 2 * far),
            pltpu.SemaphoreType.DMA((7, max(cols, 6))),
            pltpu.SemaphoreType.DMA((7, max(cols, 6))),
        ],
        compiler_params=pltpu.CompilerParams(
            collective_id=1, has_side_effects=True, vmem_limit_bytes=56 * 2**20
        ),
        name="filter_block",
    )(levels, start_block)


def body(levels, start_block):
    own_cols, rows = start_block.shape[:2]
    grid_shape = start_block.shape
    vecs = lax.axis_size("vec")
    vec = lax.axis_index("vec")
    voxel_total = lax.axis_size("brick") * rows * grid_shape[2] * grid_shape[3]
    block = own_cols * vecs
    x, x_other, y, y_other, tile = fused(levels, start_block)
    first = vec == 0
    sums = all_sum(tile)
    pairs = sums[:, :, : 6 * own_cols].reshape(vecs, own_cols, 3, 2, own_cols)
    turned = jnp.stack([pairs[0], pairs[1, :, :, ::-1]])
    sums = turned.reshape(block, 3, block)
    g00 = sums[:, 0]
    g10 = sums[:, 1]
    g11 = jnp.tril(sums[:, 2])
    g11 = g11 + jnp.tril(g11, -1).T
    gram = jnp.concatenate(
        [jnp.concatenate([g00, g10.T], axis=1), jnp.concatenate([g10, g11], axis=1)], axis=0
    )
    factor = jnp.linalg.cholesky(gram)
    inverse = lax.linalg.triangular_solve(
        factor, jnp.eye(2 * block, dtype=jnp.float32), left_side=True, lower=True
    )
    mixed = jnp.dot(inverse[:block, :block], factor[block:], precision=highest)
    alpha, beta = mixed[:, :block], mixed[:, block:]
    coeffs = lax.dynamic_slice_in_dim(inverse, block + vec * own_cols, own_cols, 0)
    coeffs = coeffs * math.sqrt(voxel_total)
    basis = combine(coeffs, vec, x, x_other, y, y_other)
    return alpha[None], beta[None], basis


def combine_kernel(coeff_ref, x_ref, xo_ref, y_ref, yo_ref, out_ref):
    cols, rows = out_ref.shape[:2]

    def one(r, carry):
        total = [jnp.zeros(out_ref.shape[2:], jnp.float32) for _ in range(cols)]
        for part, ref in enumerate((x_ref, xo_ref, y_ref, yo_ref)):
            for j in range(cols):
                value = ref[j, r]
                for i in range(cols):
                    total[i] = total[i] + coeff_ref[i, part * cols + j] * value
        for i in range(cols):
            out_ref[i, r] = total[i]
        return carry

    lax.fori_loop(0, rows, one, 0)


def combine(coeffs, vec, x, x_other, y, y_other):
    cols, rows, ny, nz = x.shape
    parts = coeffs.reshape(cols, 2, 2, cols)
    parts = jnp.where(vec == 0, parts, parts[:, :, ::-1]).reshape(cols, 4 * cols)
    slab = math.gcd(rows, 8)
    spec = pl.BlockSpec((cols, slab, ny, nz), lambda i: (0, i, 0, 0))
    return pl.pallas_call(
        combine_kernel,
        grid=(rows // slab,),
        out_shape=jax.ShapeDtypeStruct(x.shape, jnp.float32),
        in_specs=[pl.BlockSpec(memory_space=pltpu.SMEM)] + [spec] * 4,
        out_specs=spec,
        name="combine",
    )(parts, x, x_other, y, y_other)


def solution(mesh):
    return jax.shard_map(
        body,
        mesh=mesh,
        in_specs=(P(None, "brick", None, None), P("vec", "brick", None, None)),
        out_specs=(P(), P(), P("vec", "brick", None, None)),
        check_vma=False,
    )
```

```python
import functools
import math

import jax
import jax.numpy as jnp
from jax import lax
from jax.experimental import pallas as pl
from jax.experimental.pallas import tpu as pltpu
from jax.sharding import PartitionSpec as P

offsets_cube = (1, 3, 9, 27)
deepest = 27
highest = lax.Precision.HIGHEST
MESH = pl.DeviceIdType.MESH


def sum_kernel(bricks, vecs, scale, own_ref, alpha_ref, beta_ref, out_ref, slots, send_sem, recv_sem):
    brick = lax.axis_index("brick")
    vec = lax.axis_index("vec")
    total = bricks * vecs
    me = brick * vecs + vec

    def peer(step):
        other = lax.rem(me + step, total)
        return (other // vecs, lax.rem(other, vecs))

    barrier = pltpu.get_barrier_semaphore()

    def greet(step, carry):
        pl.semaphore_signal(barrier, inc=1, device_id=peer(step), device_id_type=MESH)
        return carry

    lax.fori_loop(1, total, greet, 0)
    pl.semaphore_wait(barrier, total - 1)

    def copy_of(step):
        return pltpu.make_async_remote_copy(
            src_ref=own_ref,
            dst_ref=slots.at[me],
            send_sem=send_sem.at[step],
            recv_sem=recv_sem.at[step],
            device_id=peer(step),
            device_id_type=MESH,
        )

    def push(step, carry):
        copy_of(step).start()
        return carry

    lax.fori_loop(1, total, push, 0)
    slots[pl.ds(me, 1)] = own_ref[...][None]

    def settle(step, carry):
        copy_of(step).wait()
        return carry

    lax.fori_loop(1, total, settle, 0)
    halves = []
    for half in range(vecs):
        value = slots[half]
        for other in range(1, bricks):
            value = value + slots[other * vecs + half]
        halves.append(value)
    sums = jnp.concatenate(halves, axis=0)
    block = sums.shape[0]
    turned = jnp.concatenate(
        [sums, jnp.zeros((128 - block, 128), jnp.float32)], axis=0
    ).T
    low = lax.broadcasted_iota(jnp.int32, (block, block), 0)
    low = low >= lax.broadcasted_iota(jnp.int32, (block, block), 1)
    corner = jnp.where(
        low, sums[:, 2 * block : 3 * block], turned[2 * block : 3 * block, :block]
    )
    gram = jnp.concatenate(
        [
            jnp.concatenate([sums[:, :block], turned[block : 2 * block, :block]], axis=1),
            jnp.concatenate([sums[:, block : 2 * block], corner], axis=1),
        ],
        axis=0,
    )
    size = 2 * block
    row = lax.broadcasted_iota(jnp.int32, (size, size), 0)
    eye = (row == lax.broadcasted_iota(jnp.int32, (size, size), 1)).astype(jnp.float32)
    work = jnp.concatenate(
        [gram, eye, jnp.zeros((size, 128 - 2 * size), jnp.float32)], axis=1
    )
    place = lax.broadcasted_iota(jnp.int32, work.shape, 0)
    for k in range(size):
        root = lax.rsqrt(work[k : k + 1, k : k + 1])
        pivot = work[k : k + 1] * root
        factor = work[:, k : k + 1] * root
        work = jnp.where(
            place > k, work - factor * pivot, jnp.where(place == k, pivot, work)
        )
    mixed = lax.dot_general(
        work[:block, size : size + block],
        work[:, block:size],
        (((1,), (1,)), ((), ())),
        precision=highest,
        preferred_element_type=jnp.float32,
    )
    alpha_ref[0] = mixed[:, :block]
    beta_ref[0] = jnp.where(low, mixed[:, block:], 0.0)
    out_ref[...] = work[block:, size : 2 * size] * scale


def all_sum(tile, scale):
    bricks, vecs = lax.axis_size("brick"), lax.axis_size("vec")
    total = bricks * vecs
    block = tile.shape[0] * vecs
    return pl.pallas_call(
        functools.partial(sum_kernel, bricks, vecs, scale),
        out_shape=(
            jax.ShapeDtypeStruct((1, block, block), jnp.float32),
            jax.ShapeDtypeStruct((1, block, block), jnp.float32),
            jax.ShapeDtypeStruct((block, 2 * block), jnp.float32),
        ),
        in_specs=[pl.BlockSpec(memory_space=pltpu.VMEM)],
        out_specs=(pl.BlockSpec(memory_space=pltpu.VMEM),) * 3,
        scratch_shapes=[
            pltpu.VMEM((total,) + tile.shape, jnp.float32),
            pltpu.SemaphoreType.DMA((total,)),
            pltpu.SemaphoreType.DMA((total,)),
        ],
        compiler_params=pltpu.CompilerParams(collective_id=0, has_side_effects=True),
        name="sum_blocks",
    )(tile)


ROW_STEP = 4
X_AHEAD = 3
OVER_AHEAD = 5
LAG = 2


def fused_kernel(
    bricks, lev_ref, start_ref, x_ref, xo_ref, y_ref, yo_ref, tile_ref,
    x_low, x_high, u_one, u_two, x_weights, fore, back, root, send_sem, recv_sem,
):
    cols, rows, ny, nz = start_ref.shape
    far = deepest
    step = ROW_STEP
    brick = lax.axis_index("brick")
    vec = lax.axis_index("vec")
    has_low = brick > 0
    has_high = brick < bricks - 1
    low, high = {"brick": brick - 1}, {"brick": brick + 1}
    partner = {"vec": 1 - vec}

    def remote(src, dst, kind, slot, device):
        return pltpu.make_async_remote_copy(
            src_ref=src,
            dst_ref=dst,
            send_sem=send_sem.at[kind, slot],
            recv_sem=recv_sem.at[kind, slot],
            device_id=device,
            device_id_type=MESH,
        )

    def x_up(c):
        return remote(x_ref.at[c, pl.ds(rows - far, far)], x_low.at[c], 0, c, high)

    def x_down(c):
        return remote(x_ref.at[c, pl.ds(0, far)], x_high.at[c], 1, c, low)

    def x_over(c):
        return remote(x_ref.at[c], xo_ref.at[c], 2, c, partner)

    def u_up(c):
        return remote(u_two.at[c, pl.ds(rows, far)], u_two.at[c, pl.ds(0, far)], 3, c, high)

    def u_down(c):
        return remote(
            u_two.at[c, pl.ds(far, far)], u_two.at[c, pl.ds(far + rows, far)], 4, c, low
        )

    def y_over(c):
        return remote(y_ref.at[c], yo_ref.at[c], 5, c, partner)

    def tail_up(k):
        o = offsets_cube[k]
        return remote(
            x_weights.at[k, pl.ds(far + rows - o, o)],
            x_weights.at[k, pl.ds(far - o, o)],
            6,
            k,
            high,
        )

    def root_up():
        return remote(root.at[pl.ds(rows, far)], root.at[pl.ds(0, far)], 6, 4, high)

    def root_down():
        return remote(root.at[pl.ds(far, far)], root.at[pl.ds(far + rows, far)], 6, 5, low)

    barrier = pltpu.get_barrier_semaphore()

    def greet(device):
        pl.semaphore_signal(barrier, inc=1, device_id=device, device_id_type=MESH)

    greet(partner)
    pl.when(has_low)(lambda: greet(low))
    pl.when(has_high)(lambda: greet(high))

    def weights_of(channel, place):
        return (lev_ref[channel, place].astype(jnp.float32) + 0.5) * (1.0 / 256.0)

    def prepare_x(r, carry):
        place = pl.ds(r * step, step)
        for k in range(4):
            x_weights[k, pl.ds(far + r * step, step)] = weights_of(k, place)
        return carry

    lax.fori_loop(0, rows // step, prepare_x, 0)

    def cast(c, carry):
        x_ref[c] = start_ref[c].astype(jnp.float32)
        return carry

    lax.fori_loop(0, cols, cast, 0)
    pl.semaphore_wait(
        barrier, 1 + jnp.where(has_low, 1, 0) + jnp.where(has_high, 1, 0)
    )

    @pl.when(has_high)
    def _():
        for k in range(4):
            tail_up(k).start()

    def push_x(c):
        pl.when(has_high)(lambda: x_up(c).start())
        pl.when(has_low)(lambda: x_down(c).start())

    for c in range(min(OVER_AHEAD, cols)):
        if c < X_AHEAD:
            push_x(c)
        x_over(c).start()

    edge = jnp.zeros((far, ny, nz), jnp.float32)

    @pl.when(jnp.logical_not(has_low))
    def _():
        root[pl.ds(0, far)] = edge
        for k in range(4):
            x_weights[k, pl.ds(0, far)] = edge
        for c in range(cols):
            x_low[c] = edge
            u_two[c, pl.ds(0, far)] = edge

    @pl.when(jnp.logical_not(has_high))
    def _():
        root[pl.ds(far + rows, far)] = edge
        for c in range(cols):
            x_high[c] = edge
            u_two[c, pl.ds(far + rows, far)] = edge

    lane = (step, ny, nz)
    along = [lax.broadcasted_iota(jnp.int32, lane, axis) for axis in range(3)]

    def prepare_rest(r, carry):
        place = pl.ds(r * step, step)
        degree = jnp.ones(lane, jnp.float32)
        for axis, length in ((1, ny), (2, nz)):
            for k, o in enumerate(offsets_cube):
                if o >= length:
                    continue
                channel = 4 * (axis - 1) + k
                weight = weights_of(channel + 4, place)
                forward = jnp.where(along[axis] < length - o, weight, 0.0)
                backward = pltpu.roll(forward, o, axis)
                fore[channel, place] = forward
                back[channel, place] = backward
                degree = degree + forward + backward
        root[pl.ds(far + r * step, step)] = degree
        return carry

    lax.fori_loop(0, rows // step, prepare_rest, 0)

    @pl.when(has_low)
    def _():
        for k in range(4):
            tail_up(k).wait_recv()

    limit = jnp.where(has_high, rows + far + 1, rows)

    def prepare_root(r, carry):
        place = pl.ds(far + r * step, step)
        degree = root[place]
        for k, o in enumerate(offsets_cube):
            inside = along[0] + (r * step + o) < limit
            degree = degree + jnp.where(inside, x_weights[k, place], 0.0)
            degree = degree + x_weights[k, pl.ds(far + r * step - o, step)]
        root[place] = lax.rsqrt(degree)
        return carry

    lax.fori_loop(0, rows // step, prepare_root, 0)
    pl.when(has_high)(lambda: root_up().start())
    pl.when(has_low)(lambda: root_down().start())

    def stencil(u_ref, r):
        at = far + r * step
        center = u_ref[pl.ds(at, step)]
        total = jnp.zeros(lane, jnp.float32)
        for k, o in enumerate(offsets_cube):
            total = total + x_weights[k, pl.ds(at, step)] * u_ref[pl.ds(at + o, step)]
            total = total + x_weights[k, pl.ds(at - o, step)] * u_ref[pl.ds(at - o, step)]
        place = pl.ds(r * step, step)
        for axis, length in ((1, ny), (2, nz)):
            for k, o in enumerate(offsets_cube):
                if o >= length:
                    continue
                channel = 4 * (axis - 1) + k
                total = total + fore[channel, place] * pltpu.roll(center, length - o, axis)
                total = total + back[channel, place] * pltpu.roll(center, o, axis)
        return root[pl.ds(at, step)] * total

    pl.when(has_low)(lambda: root_up().wait_recv())
    pl.when(has_high)(lambda: root_down().wait_recv())

    def first_half(c):
        pl.when(c + X_AHEAD < cols)(lambda: push_x(c + X_AHEAD))
        pl.when(c + OVER_AHEAD < cols)(lambda: x_over(c + OVER_AHEAD).start())
        u_one[pl.ds(far, rows)] = root[pl.ds(far, rows)] * x_ref[c]
        pl.when(has_low)(lambda: x_up(c).wait_recv())
        u_one[pl.ds(0, far)] = root[pl.ds(0, far)] * x_low[c]
        pl.when(has_high)(lambda: x_down(c).wait_recv())
        u_one[pl.ds(far + rows, far)] = root[pl.ds(far + rows, far)] * x_high[c]

        def one(r, inner):
            place = pl.ds(r * step, step)
            image = 0.5 * (x_ref[c, place] + stencil(u_one, r))
            y_ref[c, place] = image
            at = pl.ds(far + r * step, step)
            u_two[c, at] = root[at] * image
            return inner

        lax.fori_loop(0, rows // step, one, 0)
        pl.when(has_high)(lambda: u_up(c).start())
        pl.when(has_low)(lambda: u_down(c).start())

    column = lax.broadcasted_iota(jnp.int32, tile_ref.shape, 1)

    own_base = vec * cols
    other_base = (1 - vec) * cols

    def product(left_ref, right_ref, base, tile, j):
        def add(r, total):
            return total + left_ref[:, r] * right_ref[j, r][None]

        total = lax.fori_loop(
            0, rows, add, jnp.zeros((cols, ny, nz), jnp.float32), unroll=2
        )
        value = jnp.sum(jnp.sum(total, axis=1), axis=1, keepdims=True)
        return jnp.where(column == base + j, value, tile)

    def products(left_ref, right_ref, base, tile, ready=None):
        def one(j, tile):
            if ready is not None:
                ready(j)
            return product(left_ref, right_ref, base, tile, j)

        return lax.fori_loop(0, cols, one, tile)

    def second_half(c):
        pl.when(has_low)(lambda: u_up(c).wait_recv())
        pl.when(has_high)(lambda: u_down(c).wait_recv())

        def one(r, inner):
            place = pl.ds(r * step, step)
            y_ref[c, place] = 0.5 * (y_ref[c, place] + stencil(u_two.at[c], r))
            return inner

        lax.fori_loop(0, rows // step, one, 0)
        pl.when(vec == 0)(lambda: y_over(c).start())

    tile_ref[...] = jnp.zeros(tile_ref.shape, jnp.float32)

    def turn(c, carry):
        pl.when(c < cols)(lambda: first_half(c))
        pl.when(c >= LAG)(lambda: second_half(c - LAG))

        @pl.when(c < cols)
        def _():
            tile_ref[...] = product(x_ref, x_ref, own_base, tile_ref[...], c)

        return carry

    lax.fori_loop(0, cols + LAG, turn, 0)
    block = 2 * cols
    tile = tile_ref[...]
    tile = products(x_ref, xo_ref, other_base, tile, lambda j: x_over(j).wait_recv())
    tile = products(y_ref, x_ref, block + own_base, tile)
    tile = products(y_ref, xo_ref, block + other_base, tile)
    tile = products(y_ref, y_ref, 2 * block + own_base, tile)
    tile_ref[...] = tile

    @pl.when(vec == 1)
    def _():
        tile_ref[...] = products(
            y_ref, yo_ref, 2 * block + other_base, tile_ref[...], lambda j: y_over(j).wait_recv()
        )

    @pl.when(vec == 0)
    def _():
        for c in range(cols):
            yo_ref[c] = jnp.zeros((rows, ny, nz), jnp.float32)

    def finish(c, carry):
        x_over(c).wait_send()

        @pl.when(has_high)
        def _():
            x_up(c).wait_send()
            u_up(c).wait_send()

        @pl.when(has_low)
        def _():
            x_down(c).wait_send()
            u_down(c).wait_send()

        pl.when(vec == 0)(lambda: y_over(c).wait_send())
        return carry

    lax.fori_loop(0, cols, finish, 0)

    @pl.when(has_high)
    def _():
        for k in range(4):
            tail_up(k).wait_send()
        root_up().wait_send()

    pl.when(has_low)(lambda: root_down().wait_send())


def fused(levels, start_block):
    cols, rows, ny, nz = start_block.shape
    far = deepest
    field = jax.ShapeDtypeStruct(start_block.shape, jnp.float32)
    in_vmem = pl.BlockSpec(memory_space=pltpu.VMEM)
    plane = (ny, nz)

    def room(*lead):
        return pltpu.VMEM(lead + plane, jnp.float32)

    return pl.pallas_call(
        functools.partial(fused_kernel, lax.axis_size("brick")),
        out_shape=(field,) * 4 + (jax.ShapeDtypeStruct((cols, 128), jnp.float32),),
        in_specs=[in_vmem] * 2,
        out_specs=(in_vmem,) * 5,
        scratch_shapes=[
            room(cols, far),
            room(cols, far),
            room(rows + 2 * far),
            room(cols, rows + 2 * far),
            room(4, rows + far),
            room(8, rows),
            room(8, rows),
            room(rows + 2 * far),
            pltpu.SemaphoreType.DMA((7, max(cols, 6))),
            pltpu.SemaphoreType.DMA((7, max(cols, 6))),
        ],
        compiler_params=pltpu.CompilerParams(
            collective_id=1, has_side_effects=True, vmem_limit_bytes=56 * 2**20
        ),
        name="filter_block",
    )(levels, start_block)


def body(levels, start_block):
    rows = start_block.shape[1]
    grid_shape = start_block.shape
    voxel_total = lax.axis_size("brick") * rows * grid_shape[2] * grid_shape[3]
    x, x_other, y, y_other, tile = fused(levels, start_block)
    alpha, beta, coeffs = all_sum(tile, math.sqrt(voxel_total))
    return alpha, beta, combine(coeffs, x, x_other, y, y_other)


def combine_kernel(coeff_ref, x_ref, xo_ref, y_ref, yo_ref, out_ref):
    cols, rows = out_ref.shape[:2]
    first = lax.axis_index("vec") * cols
    second = cols - first
    begins = (first, second, 2 * cols + first, 2 * cols + second)

    def one(r, carry):
        total = [jnp.zeros(out_ref.shape[2:], jnp.float32) for _ in range(cols)]
        for part, ref in enumerate((x_ref, xo_ref, y_ref, yo_ref)):
            for j in range(cols):
                value = ref[j, r]
                for i in range(cols):
                    total[i] = total[i] + coeff_ref[first + i, begins[part] + j] * value
        for i in range(cols):
            out_ref[i, r] = total[i]
        return carry

    lax.fori_loop(0, rows, one, 0)


def combine(coeffs, x, x_other, y, y_other):
    cols, rows, ny, nz = x.shape
    slab = math.gcd(rows, 8)
    spec = pl.BlockSpec((cols, slab, ny, nz), lambda i: (0, i, 0, 0))
    return pl.pallas_call(
        combine_kernel,
        grid=(rows // slab,),
        out_shape=jax.ShapeDtypeStruct(x.shape, jnp.float32),
        in_specs=[pl.BlockSpec(memory_space=pltpu.SMEM)] + [spec] * 4,
        out_specs=spec,
        name="combine",
    )(coeffs, x, x_other, y, y_other)


def solution(mesh):
    return jax.shard_map(
        body,
        mesh=mesh,
        in_specs=(P(None, "brick", None, None), P("vec", "brick", None, None)),
        out_specs=(P(), P(), P("vec", "brick", None, None)),
        check_vma=False,
    )
```

```python
import functools
import math

import jax
import jax.numpy as jnp
from jax import lax
from jax.experimental import pallas as pl
from jax.experimental.pallas import tpu as pltpu
from jax.sharding import PartitionSpec as P

offsets_cube = (1, 3, 9, 27)
deepest = 27
highest = lax.Precision.HIGHEST
MESH = pl.DeviceIdType.MESH


def sum_kernel(bricks, vecs, scale, own_ref, alpha_ref, beta_ref, out_ref, slots, send_sem, recv_sem):
    brick = lax.axis_index("brick")
    vec = lax.axis_index("vec")
    total = bricks * vecs
    me = brick * vecs + vec

    def peer(step):
        other = lax.rem(me + step, total)
        return (other // vecs, lax.rem(other, vecs))

    barrier = pltpu.get_barrier_semaphore()

    def greet(step, carry):
        pl.semaphore_signal(barrier, inc=1, device_id=peer(step), device_id_type=MESH)
        return carry

    lax.fori_loop(1, total, greet, 0)
    pl.semaphore_wait(barrier, total - 1)

    def copy_of(step):
        return pltpu.make_async_remote_copy(
            src_ref=own_ref,
            dst_ref=slots.at[me],
            send_sem=send_sem.at[step],
            recv_sem=recv_sem.at[step],
            device_id=peer(step),
            device_id_type=MESH,
        )

    def push(step, carry):
        copy_of(step).start()
        return carry

    lax.fori_loop(1, total, push, 0)
    slots[pl.ds(me, 1)] = own_ref[...][None]

    def settle(step, carry):
        copy_of(step).wait()
        return carry

    lax.fori_loop(1, total, settle, 0)
    halves = []
    for half in range(vecs):
        value = slots[half]
        for other in range(1, bricks):
            value = value + slots[other * vecs + half]
        halves.append(value)
    sums = jnp.concatenate(halves, axis=0)
    block = sums.shape[0]
    turned = jnp.concatenate(
        [sums, jnp.zeros((128 - block, 128), jnp.float32)], axis=0
    ).T
    low = lax.broadcasted_iota(jnp.int32, (block, block), 0)
    low = low >= lax.broadcasted_iota(jnp.int32, (block, block), 1)
    corner = jnp.where(
        low, sums[:, 2 * block : 3 * block], turned[2 * block : 3 * block, :block]
    )
    gram = jnp.concatenate(
        [
            jnp.concatenate([sums[:, :block], turned[block : 2 * block, :block]], axis=1),
            jnp.concatenate([sums[:, block : 2 * block], corner], axis=1),
        ],
        axis=0,
    )
    size = 2 * block
    row = lax.broadcasted_iota(jnp.int32, (size, size), 0)
    eye = (row == lax.broadcasted_iota(jnp.int32, (size, size), 1)).astype(jnp.float32)
    work = jnp.concatenate(
        [gram, eye, jnp.zeros((size, 128 - 2 * size), jnp.float32)], axis=1
    )
    place = lax.broadcasted_iota(jnp.int32, work.shape, 0)
    for k in range(size):
        root = lax.rsqrt(work[k : k + 1, k : k + 1])
        pivot = work[k : k + 1] * root
        factor = work[:, k : k + 1] * root
        work = jnp.where(
            place > k, work - factor * pivot, jnp.where(place == k, pivot, work)
        )
    mixed = lax.dot_general(
        work[:block, size : size + block],
        work[:, block:size],
        (((1,), (1,)), ((), ())),
        precision=highest,
        preferred_element_type=jnp.float32,
    )
    alpha_ref[0] = mixed[:, :block]
    beta_ref[0] = jnp.where(low, mixed[:, block:], 0.0)
    cols = block // 2
    first = vec == 0
    rest = jnp.where(first, work[block : block + cols], work[block + cols :])
    rest = rest[:, size : 2 * size] * scale
    order = [1, 0, 3, 2]
    swapped = [rest[:, p * cols : (p + 1) * cols] for p in order]
    out_ref[...] = jnp.where(first, rest, jnp.concatenate(swapped, axis=1))


def all_sum(tile, scale):
    bricks, vecs = lax.axis_size("brick"), lax.axis_size("vec")
    total = bricks * vecs
    block = tile.shape[0] * vecs
    return pl.pallas_call(
        functools.partial(sum_kernel, bricks, vecs, scale),
        out_shape=(
            jax.ShapeDtypeStruct((1, block, block), jnp.float32),
            jax.ShapeDtypeStruct((1, block, block), jnp.float32),
            jax.ShapeDtypeStruct((block // 2, 2 * block), jnp.float32),
        ),
        in_specs=[pl.BlockSpec(memory_space=pltpu.VMEM)],
        out_specs=(pl.BlockSpec(memory_space=pltpu.VMEM),) * 3,
        scratch_shapes=[
            pltpu.VMEM((total,) + tile.shape, jnp.float32),
            pltpu.SemaphoreType.DMA((total,)),
            pltpu.SemaphoreType.DMA((total,)),
        ],
        compiler_params=pltpu.CompilerParams(collective_id=0, has_side_effects=True),
        name="sum_blocks",
    )(tile)


ROW_STEP = 4
X_AHEAD = 3
OVER_AHEAD = 5
LAG = 2


def fused_kernel(
    bricks, lev_ref, start_ref, x_ref, xo_ref, y_ref, yo_ref, tile_ref,
    x_low, x_high, u_one, u_two, x_weights, fore, back, root, send_sem, recv_sem,
):
    cols, rows, ny, nz = start_ref.shape
    far = deepest
    step = ROW_STEP
    brick = lax.axis_index("brick")
    vec = lax.axis_index("vec")
    has_low = brick > 0
    has_high = brick < bricks - 1
    low, high = {"brick": brick - 1}, {"brick": brick + 1}
    partner = {"vec": 1 - vec}

    def remote(src, dst, kind, slot, device):
        return pltpu.make_async_remote_copy(
            src_ref=src,
            dst_ref=dst,
            send_sem=send_sem.at[kind, slot],
            recv_sem=recv_sem.at[kind, slot],
            device_id=device,
            device_id_type=MESH,
        )

    def x_up(c):
        return remote(x_ref.at[c, pl.ds(rows - far, far)], x_low.at[c], 0, c, high)

    def x_down(c):
        return remote(x_ref.at[c, pl.ds(0, far)], x_high.at[c], 1, c, low)

    def x_over(c):
        return remote(x_ref.at[c], xo_ref.at[c], 2, c, partner)

    def u_up(c):
        return remote(u_two.at[c, pl.ds(rows, far)], u_two.at[c, pl.ds(0, far)], 3, c, high)

    def u_down(c):
        return remote(
            u_two.at[c, pl.ds(far, far)], u_two.at[c, pl.ds(far + rows, far)], 4, c, low
        )

    def y_over(c):
        return remote(y_ref.at[c], yo_ref.at[c], 5, c, partner)

    def tail_up(k):
        o = offsets_cube[k]
        return remote(
            x_weights.at[k, pl.ds(far + rows - o, o)],
            x_weights.at[k, pl.ds(far - o, o)],
            6,
            k,
            high,
        )

    def root_up():
        return remote(root.at[pl.ds(rows, far)], root.at[pl.ds(0, far)], 6, 4, high)

    def root_down():
        return remote(root.at[pl.ds(far, far)], root.at[pl.ds(far + rows, far)], 6, 5, low)

    barrier = pltpu.get_barrier_semaphore()

    def greet(device):
        pl.semaphore_signal(barrier, inc=1, device_id=device, device_id_type=MESH)

    greet(partner)
    pl.when(has_low)(lambda: greet(low))
    pl.when(has_high)(lambda: greet(high))

    def weights_of(channel, place):
        return (lev_ref[channel, place].astype(jnp.float32) + 0.5) * (1.0 / 256.0)

    def prepare_x(r, carry):
        place = pl.ds(r * step, step)
        for k in range(4):
            x_weights[k, pl.ds(far + r * step, step)] = weights_of(k, place)
        return carry

    lax.fori_loop(0, rows // step, prepare_x, 0)

    def cast(c, carry):
        x_ref[c] = start_ref[c].astype(jnp.float32)
        return carry

    lax.fori_loop(0, cols, cast, 0)
    pl.semaphore_wait(
        barrier, 1 + jnp.where(has_low, 1, 0) + jnp.where(has_high, 1, 0)
    )

    @pl.when(has_high)
    def _():
        for k in range(4):
            tail_up(k).start()

    def push_x(c):
        pl.when(has_high)(lambda: x_up(c).start())
        pl.when(has_low)(lambda: x_down(c).start())

    for c in range(min(OVER_AHEAD, cols)):
        if c < X_AHEAD:
            push_x(c)
        x_over(c).start()

    edge = jnp.zeros((far, ny, nz), jnp.float32)

    @pl.when(jnp.logical_not(has_low))
    def _():
        root[pl.ds(0, far)] = edge
        for k in range(4):
            x_weights[k, pl.ds(0, far)] = edge
        for c in range(cols):
            x_low[c] = edge
            u_two[c, pl.ds(0, far)] = edge

    @pl.when(jnp.logical_not(has_high))
    def _():
        root[pl.ds(far + rows, far)] = edge
        for c in range(cols):
            x_high[c] = edge
            u_two[c, pl.ds(far + rows, far)] = edge

    lane = (step, ny, nz)
    along = [lax.broadcasted_iota(jnp.int32, lane, axis) for axis in range(3)]

    def prepare_rest(r, carry):
        place = pl.ds(r * step, step)
        degree = jnp.ones(lane, jnp.float32)
        for axis, length in ((1, ny), (2, nz)):
            for k, o in enumerate(offsets_cube):
                if o >= length:
                    continue
                channel = 4 * (axis - 1) + k
                weight = weights_of(channel + 4, place)
                forward = jnp.where(along[axis] < length - o, weight, 0.0)
                backward = pltpu.roll(forward, o, axis)
                fore[channel, place] = forward
                back[channel, place] = backward
                degree = degree + forward + backward
        root[pl.ds(far + r * step, step)] = degree
        return carry

    lax.fori_loop(0, rows // step, prepare_rest, 0)

    @pl.when(has_low)
    def _():
        for k in range(4):
            tail_up(k).wait_recv()

    limit = jnp.where(has_high, rows + far + 1, rows)

    def prepare_root(r, carry):
        place = pl.ds(far + r * step, step)
        degree = root[place]
        for k, o in enumerate(offsets_cube):
            inside = along[0] + (r * step + o) < limit
            degree = degree + jnp.where(inside, x_weights[k, place], 0.0)
            degree = degree + x_weights[k, pl.ds(far + r * step - o, step)]
        root[place] = lax.rsqrt(degree)
        return carry

    lax.fori_loop(0, rows // step, prepare_root, 0)
    pl.when(has_high)(lambda: root_up().start())
    pl.when(has_low)(lambda: root_down().start())

    def stencil(u_ref, r):
        at = far + r * step
        center = u_ref[pl.ds(at, step)]
        total = jnp.zeros(lane, jnp.float32)
        for k, o in enumerate(offsets_cube):
            total = total + x_weights[k, pl.ds(at, step)] * u_ref[pl.ds(at + o, step)]
            total = total + x_weights[k, pl.ds(at - o, step)] * u_ref[pl.ds(at - o, step)]
        place = pl.ds(r * step, step)
        for axis, length in ((1, ny), (2, nz)):
            for k, o in enumerate(offsets_cube):
                if o >= length:
                    continue
                channel = 4 * (axis - 1) + k
                total = total + fore[channel, place] * pltpu.roll(center, length - o, axis)
                total = total + back[channel, place] * pltpu.roll(center, o, axis)
        return root[pl.ds(at, step)] * total

    pl.when(has_low)(lambda: root_up().wait_recv())
    pl.when(has_high)(lambda: root_down().wait_recv())

    def first_half(c):
        pl.when(c + X_AHEAD < cols)(lambda: push_x(c + X_AHEAD))
        pl.when(c + OVER_AHEAD < cols)(lambda: x_over(c + OVER_AHEAD).start())
        u_one[pl.ds(far, rows)] = root[pl.ds(far, rows)] * x_ref[c]
        pl.when(has_low)(lambda: x_up(c).wait_recv())
        u_one[pl.ds(0, far)] = root[pl.ds(0, far)] * x_low[c]
        pl.when(has_high)(lambda: x_down(c).wait_recv())
        u_one[pl.ds(far + rows, far)] = root[pl.ds(far + rows, far)] * x_high[c]

        def one(r, inner):
            place = pl.ds(r * step, step)
            image = 0.5 * (x_ref[c, place] + stencil(u_one, r))
            y_ref[c, place] = image
            at = pl.ds(far + r * step, step)
            u_two[c, at] = root[at] * image
            return inner

        lax.fori_loop(0, rows // step, one, 0)
        pl.when(has_high)(lambda: u_up(c).start())
        pl.when(has_low)(lambda: u_down(c).start())

    column = lax.broadcasted_iota(jnp.int32, tile_ref.shape, 1)

    own_base = vec * cols
    other_base = (1 - vec) * cols

    def product(left_ref, right_ref, base, tile, j):
        def add(r, total):
            return total + left_ref[:, r] * right_ref[j, r][None]

        total = lax.fori_loop(
            0, rows, add, jnp.zeros((cols, ny, nz), jnp.float32), unroll=2
        )
        value = jnp.sum(jnp.sum(total, axis=1), axis=1, keepdims=True)
        return jnp.where(column == base + j, value, tile)

    def products(left_ref, right_ref, base, tile, ready=None):
        def one(j, tile):
            if ready is not None:
                ready(j)
            return product(left_ref, right_ref, base, tile, j)

        return lax.fori_loop(0, cols, one, tile)

    def second_half(c):
        pl.when(has_low)(lambda: u_up(c).wait_recv())
        pl.when(has_high)(lambda: u_down(c).wait_recv())

        def one(r, inner):
            place = pl.ds(r * step, step)
            y_ref[c, place] = 0.5 * (y_ref[c, place] + stencil(u_two.at[c], r))
            return inner

        lax.fori_loop(0, rows // step, one, 0)
        pl.when(vec == 0)(lambda: y_over(c).start())

    tile_ref[...] = jnp.zeros(tile_ref.shape, jnp.float32)

    def turn(c, carry):
        pl.when(c < cols)(lambda: first_half(c))
        pl.when(c >= LAG)(lambda: second_half(c - LAG))

        @pl.when(c < cols)
        def _():
            tile_ref[...] = product(x_ref, x_ref, own_base, tile_ref[...], c)

        @pl.when(c >= LAG)
        def _():
            x_over(c - LAG).wait_recv()
            tile_ref[...] = product(x_ref, xo_ref, other_base, tile_ref[...], c - LAG)

        return carry

    lax.fori_loop(0, cols + LAG, turn, 0)
    block = 2 * cols
    tile = tile_ref[...]
    tile = products(y_ref, x_ref, block + own_base, tile)
    tile = products(y_ref, xo_ref, block + other_base, tile)
    tile = products(y_ref, y_ref, 2 * block + own_base, tile)
    tile_ref[...] = tile

    @pl.when(vec == 1)
    def _():
        tile_ref[...] = products(
            y_ref, yo_ref, 2 * block + other_base, tile_ref[...], lambda j: y_over(j).wait_recv()
        )

    @pl.when(vec == 0)
    def _():
        for c in range(cols):
            yo_ref[c] = jnp.zeros((rows, ny, nz), jnp.float32)

    def finish(c, carry):
        x_over(c).wait_send()

        @pl.when(has_high)
        def _():
            x_up(c).wait_send()
            u_up(c).wait_send()

        @pl.when(has_low)
        def _():
            x_down(c).wait_send()
            u_down(c).wait_send()

        pl.when(vec == 0)(lambda: y_over(c).wait_send())
        return carry

    lax.fori_loop(0, cols, finish, 0)

    @pl.when(has_high)
    def _():
        for k in range(4):
            tail_up(k).wait_send()
        root_up().wait_send()

    pl.when(has_low)(lambda: root_down().wait_send())


def fused(levels, start_block):
    cols, rows, ny, nz = start_block.shape
    far = deepest
    field = jax.ShapeDtypeStruct(start_block.shape, jnp.float32)
    in_vmem = pl.BlockSpec(memory_space=pltpu.VMEM)
    plane = (ny, nz)

    def room(*lead):
        return pltpu.VMEM(lead + plane, jnp.float32)

    return pl.pallas_call(
        functools.partial(fused_kernel, lax.axis_size("brick")),
        out_shape=(field,) * 4 + (jax.ShapeDtypeStruct((cols, 128), jnp.float32),),
        in_specs=[in_vmem] * 2,
        out_specs=(in_vmem,) * 5,
        scratch_shapes=[
            room(cols, far),
            room(cols, far),
            room(rows + 2 * far),
            room(cols, rows + 2 * far),
            room(4, rows + far),
            room(8, rows),
            room(8, rows),
            room(rows + 2 * far),
            pltpu.SemaphoreType.DMA((7, max(cols, 6))),
            pltpu.SemaphoreType.DMA((7, max(cols, 6))),
        ],
        compiler_params=pltpu.CompilerParams(
            collective_id=1, has_side_effects=True, vmem_limit_bytes=56 * 2**20
        ),
        name="filter_block",
    )(levels, start_block)


def body(levels, start_block):
    rows = start_block.shape[1]
    grid_shape = start_block.shape
    voxel_total = lax.axis_size("brick") * rows * grid_shape[2] * grid_shape[3]
    x, x_other, y, y_other, tile = fused(levels, start_block)
    alpha, beta, coeffs = all_sum(tile, math.sqrt(voxel_total))
    return alpha, beta, combine(coeffs, x, x_other, y, y_other)


def combine_kernel(coeff_ref, x_ref, xo_ref, y_ref, yo_ref, out_ref):
    cols, rows = out_ref.shape[:2]
    pair = math.gcd(rows, 2)

    def one(r, carry):
        place = pl.ds(r * pair, pair)
        total = [jnp.zeros((pair,) + out_ref.shape[2:], jnp.float32) for _ in range(cols)]
        for part, ref in enumerate((x_ref, xo_ref, y_ref, yo_ref)):
            for j in range(cols):
                value = ref[j, place]
                for i in range(cols):
                    total[i] = total[i] + coeff_ref[i, part * cols + j] * value
        for i in range(cols):
            out_ref[i, place] = total[i]
        return carry

    lax.fori_loop(0, rows // pair, one, 0)


def combine(coeffs, x, x_other, y, y_other):
    cols, rows, ny, nz = x.shape
    slab = math.gcd(rows, 8)
    spec = pl.BlockSpec((cols, slab, ny, nz), lambda i: (0, i, 0, 0))
    return pl.pallas_call(
        combine_kernel,
        grid=(rows // slab,),
        out_shape=jax.ShapeDtypeStruct(x.shape, jnp.float32),
        in_specs=[pl.BlockSpec(memory_space=pltpu.SMEM)] + [spec] * 4,
        out_specs=spec,
        name="combine",
    )(coeffs, x, x_other, y, y_other)


def solution(mesh):
    return jax.shard_map(
        body,
        mesh=mesh,
        in_specs=(P(None, "brick", None, None), P("vec", "brick", None, None)),
        out_specs=(P(), P(), P("vec", "brick", None, None)),
        check_vma=False,
    )
```
